32 devices in a mesh: groups: 2 (over y), seq: 4 (over z), dp: 2 (over x), head: 2 (over core).
Axes of the slice: x: 2, y: 2, z: 4, core: 2. Of those that a mesh axis runs over, the one named last changes fastest.
Arguments:
- latents: bfloat16 [4, 8, 512, 1024], P(('groups', 'dp'), None, 'seq', 'head'), parts along dimension 0, may hold values from -6 to 6
- log_decay: bfloat16 [4, 8, 512, 8], P(('groups', 'dp'), None, 'seq', 'head'), parts along dimension 0, may hold values from -1 to 0, as said below
- seg_lengths: int32 [4, 4], P(('groups', 'dp')), parts along dimension 0, may hold values from 1 to 2048, 4096 in all within a row
- qkv_weight: bfloat16 [1024, 3, 1024], P('seq', None, 'head'), may hold values from -0.1875 to 0.1875
- out_weight: bfloat16 [1024, 1024], P('seq', 'head'), may hold values from -0.1875 to 0.1875
- cotangent: bfloat16 [4, 8, 512, 1024], P(('groups', 'dp'), 'seq', None, 'head'), parts along dimension 0, may hold values from -6 to 6
Outputs:
- layer_out: bfloat16 [4, 8, 512, 1024], P(('groups', 'dp'), 'seq', None, 'head'), parts along dimension 0
- output_weight_gradient: float32 [2048, 1024], P(('groups', 'seq'), 'head'), parts along dimension 0
The draws below stay inside these ranges and needn't reach their ends.
There are 2 independent parts, one for each index of `groups`. The reference program is written for one: setup_inputs(seed, part) draws one part's arguments, and reference() takes and returns one part's arrays. A program takes and returns all parts, laid end to end along the dimension named above; an argument that names none is the same for every part. Nothing has to cross between parts.
Inputs may be any that keep to these rules, and one draw needn't show every extreme that they name: `log_decay`: never positive. `seg_lengths`: each row sums to 4096; a segment's state is reset at its first token.
All inputs are finite; a program needn't handle non-finite values.
Results may differ from the reference program's by a relative error of at most 0.0073.
Values may be sent and summed in bfloat16 or wider, within the bound.
A program may use at most 64 MiB of HBM per device.

```python
import math
import jax
import jax.numpy as jnp
import numpy as np
from jax import lax

D = 1024
H = 8
HD = 128
AZ = 512
SCAN_LINES_PER = 2
SEGS = 4
SR = 8
LEN = 4096
DRIVES = 2


def draw_log_decay(key, part):
    keys = jax.random.split(key, 7)
    share = 0.5
    quick = jax.random.uniform(keys[0], (DRIVES, 1, 1, H)) < share
    fast_rate = jnp.exp(jax.random.uniform(keys[1], (DRIVES, 1, 1, H), minval=math.log(1.0 / 50.0), maxval=math.log(1.0 / 30.0)))
    slow_rate = jnp.exp(jax.random.uniform(keys[2], (DRIVES, 1, 1, H), minval=math.log(0.02), maxval=math.log(0.3))) * (math.log(10.0) / LEN)
    nominal_speed = jnp.where(quick, fast_rate, slow_rate)
    blocks = SR // SCAN_LINES_PER
    nearby_scaling = jnp.exp(jax.random.uniform(keys[3], (DRIVES, blocks, 1, H), minval=-0.69, maxval=0.69))
    nearby_scaling = jnp.repeat(nearby_scaling, SCAN_LINES_PER, axis=1)
    rough_estimate = jax.random.uniform(keys[4], (DRIVES, SR, AZ, H), minval=0.5, maxval=1.5)
    spots = jax.random.randint(keys[5], (DRIVES, 3), 0, LEN)
    place = jnp.arange(SR, dtype=jnp.int32)[:, None] * AZ + jnp.arange(AZ, dtype=jnp.int32)[None, :]
    excluded_flags = jnp.any(place[None, None, :, :] == spots[:, :, None, None], axis=1)
    objective_terms = jnp.log(jax.random.uniform(keys[6], (DRIVES, SR, AZ, H), minval=0.5, maxval=0.8))
    spike_clusters = jnp.where(excluded_flags[:, :, :, None], objective_terms, 0.0)
    return (spike_clusters - nominal_speed * nearby_scaling * rough_estimate).astype(jnp.float32).astype(jnp.bfloat16)


def level_of(rng, extent, pieces, smallest, largest):
    level = 1.0
    for dim, blocks in pieces:
        draws = jax.random.uniform(jax.random.fold_in(jax.random.fold_in(rng, 6), dim), (blocks,), jnp.float32, smallest / len(pieces), largest / len(pieces))
        level = level * jnp.repeat(jnp.exp(draws), extent[dim] // blocks).reshape((-1,) + (1,) * (len(extent) - 1 - dim))
    return level


def split_up(number_of, total, limit, lean):
    weights = [(1 << 20) // math.isqrt(grade ** lean) + 1 for grade in range(2, number_of + 1)]
    spare, holding = total - limit - (number_of - 1), [1] * (number_of - 1)
    while spare > 0:
        free = [i for i in range(number_of - 1) if holding[i] < limit]
        pool, left = sum([weights[i] for i in free]), spare
        for i in free:
            addition = min(limit - holding[i], max(1, left * weights[i] // pool), spare)
            holding[i] = holding[i] + addition
            spare = spare - addition
    return np.array([limit] + holding)


def ragged_sizes(key, number_of, total, reach, slope):
    if number_of == 2:
        one = jax.random.randint(key, (), max(1, total - reach), min(reach, total - 1) + 1)
        return jnp.stack([one, total - one])
    sizes = jnp.asarray(split_up(number_of, total, reach, slope), jnp.int32)
    twos = (number_of - 1) // 2
    source_of, taker = sizes[1:1 + 2 * twos:2], sizes[2:2 + 2 * twos:2]
    slack = jnp.minimum(source_of - 1, reach - taker)
    passed = jax.random.randint(jax.random.fold_in(key, 1), (twos,), 0, 1 << 20) % (slack + 1)
    sizes = sizes.at[1:1 + 2 * twos:2].set(source_of - passed).at[2:2 + 2 * twos:2].set(taker + passed)
    return sizes[jax.random.permutation(jax.random.fold_in(key, 2), number_of)]


def centred(rng, shape, scale, limit, cuts=(), kind=jnp.bfloat16):
    values = scale * jax.random.normal(rng, shape, jnp.float32)
    if cuts:
        values = values * level_of(rng, shape, cuts, -0.22, 0.18)
    return jnp.clip(values, -limit, limit).astype(kind)


def setup_inputs(seed: int = 0, part: int = 0) -> dict:
    seeds = jax.random.split(jax.random.key(seed), 7)
    part_keys = jax.random.split(jax.random.fold_in(seeds[6], part), 7)
    latents = centred(part_keys[0], (DRIVES, SR, AZ, D), 1.0, 6.0, ((0, 2), (2, 4), (3, 2)))
    log_decay = draw_log_decay(jax.random.fold_in(jax.random.fold_in(seeds[6], part), 71), part)
    seg_lengths = jax.vmap(lambda own: ragged_sizes(own, SEGS, LEN, LEN // 2, 1))(jax.random.split(part_keys[2], DRIVES)).reshape((DRIVES, SEGS)).astype(jnp.int32)
    qkv_weight = centred(seeds[3], (D, 3, D), D ** -0.5, 0.1875, ((0, 4), (2, 2)))
    out_weight = centred(seeds[4], (D, D), D ** -0.5, 0.1875, ((0, 4), (1, 2)))
    cotangent = centred(part_keys[5], (DRIVES, SR, AZ, D), 1.0, 6.0, ((0, 2), (1, 4), (3, 2)))
    return {"latents": latents, "log_decay": log_decay, "seg_lengths": seg_lengths, "qkv_weight": qkv_weight, "out_weight": out_weight, "cotangent": cotangent}


def block_step(carry_state, queries, key_rows, values_in, log_rates, segment, previous):
    head_scale = queries.shape[-1] ** (-0.5)
    query_f = queries.astype(jnp.float32)
    key_f = key_rows.astype(jnp.float32)
    value_f = values_in.astype(jnp.float32)
    cumulative = jnp.cumsum(log_rates, axis=-1)
    size_here = log_rates.shape[-1]
    order_idx = jnp.arange(size_here)
    allowed = (order_idx[:, None] >= order_idx[None, :]) & (segment[:, None] == segment[None, :])
    spread = cumulative[:, :, None] - cumulative[:, None, :]
    weight = jnp.where(allowed[None], jnp.exp(jnp.where(allowed[None], spread, 0.0)), 0.0)
    scores = jnp.einsum('htd,hsd->hts', query_f, key_f, precision=lax.Precision.HIGHEST)
    mixing = (scores * head_scale * weight).astype(jnp.bfloat16)
    inner_sum = jnp.einsum('hts,hsd->htd', mixing.astype(jnp.float32), value_f, precision=lax.Precision.HIGHEST)
    kept_mask = (segment == previous).astype(jnp.float32)
    carried = jnp.einsum('htd,hde->hte', query_f, carry_state, precision=lax.Precision.HIGHEST)
    result = inner_sum + kept_mask[None, :, None] * jnp.exp(cumulative)[:, :, None] * carried * head_scale
    last_seg = segment[-1]
    tail_decay = jnp.exp(cumulative[:, -1:] - cumulative) * (segment == last_seg).astype(jnp.float32)[None, :]
    decayed = (key_f * tail_decay[:, :, None]).astype(jnp.bfloat16)
    fresh = jnp.einsum('hsd,hse->hde', decayed.astype(jnp.float32), value_f, precision=lax.Precision.HIGHEST)
    through = jnp.exp(cumulative[:, -1]) * (last_seg == previous).astype(jnp.float32)
    return (through[:, None, None] * carry_state + fresh, result)

def to_blocks(array, count):
    moved = array.reshape((array.shape[0], count, array.shape[1] // count) + array.shape[2:])
    return jnp.moveaxis(moved, 1, 0)

def local_pass(queries, key_rows, values_in, log_rates, segment, before, block_size):
    heads_here, length, head_dim = queries.shape
    count = length // block_size
    seg_blocks = segment.reshape(count, block_size)
    previous = jnp.concatenate([jnp.reshape(before, (1,)).astype(jnp.int32), seg_blocks[:-1, -1].astype(jnp.int32)])

    def advance(carry_state, slab_in):
        q_blk, k_blk, v_blk, r_blk, s_blk, p_blk = slab_in
        return block_step(carry_state, q_blk, k_blk, v_blk, r_blk, s_blk, p_blk)
    start_state = jnp.zeros((heads_here, head_dim, head_dim), jnp.float32)
    final_state, block_outs = lax.scan(advance, start_state, (to_blocks(queries, count), to_blocks(key_rows, count), to_blocks(values_in, count), to_blocks(log_rates, count), seg_blocks, previous))
    outputs = jnp.moveaxis(block_outs, 0, 1).reshape(heads_here, length, head_dim)
    return (outputs, final_state)

def reference(latents, log_decay, seg_lengths, qkv_weight, out_weight, cotangent):
    block_size = min(512, SCAN_LINES_PER * AZ)

    def one_drive(inputs):
        drive_latents, drive_rates, lengths = inputs
        flat_rows = drive_latents.reshape(LEN, D)
        heads_qkv = []
        for member in range(3):
            projected = jnp.dot(flat_rows, qkv_weight[:, member, :], preferred_element_type=jnp.float32).astype(jnp.bfloat16)
            heads_qkv.append(jnp.transpose(projected.reshape(LEN, H, HD), (1, 0, 2)))
        log_rates = jnp.transpose(drive_rates.reshape(LEN, H).astype(jnp.float32))
        starts = jnp.cumsum(lengths) - lengths
        position = jnp.arange(LEN, dtype=jnp.int32)
        segment = (lax.optimization_barrier(jnp.sum((starts[:, None] <= position[None, :]).astype(jnp.int32), axis=0)) - 1).astype(jnp.int32)
        outputs, final_state = local_pass(heads_qkv[0], heads_qkv[1], heads_qkv[2], log_rates, segment, jnp.int32(-1), block_size)
        normed = outputs * lax.rsqrt(lax.optimization_barrier(jnp.mean(outputs * outputs, axis=-1, keepdims=True)) + 1e-06)
        return jnp.transpose(normed.astype(jnp.bfloat16), (1, 0, 2)).reshape(LEN, D)
    attn_all = lax.map(one_drive, (latents, log_decay, seg_lengths))
    flat_attn = attn_all.reshape(DRIVES * LEN, D)
    layer_out = jnp.dot(flat_attn, out_weight, preferred_element_type=jnp.float32).astype(jnp.bfloat16).reshape(DRIVES, SR, AZ, D)
    weight_grad = jnp.dot(flat_attn.T, cotangent.reshape(DRIVES * LEN, D), preferred_element_type=jnp.float32) * (DRIVES * LEN) ** (-0.5)
    return (layer_out, weight_grad)
```

```python
from functools import partial

import jax
import jax.numpy as jnp
from jax import lax
from jax.experimental import pallas as pl
from jax.experimental.pallas import tpu as pltpu

BF = jnp.bfloat16
F32 = jnp.float32


def remote(src, dst, send, recv, device):
    return pltpu.make_async_remote_copy(
        src_ref=src,
        dst_ref=dst,
        send_sem=send,
        recv_sem=recv,
        device_id=device,
        device_id_type=pl.DeviceIdType.MESH,
    )


def dot(a, b, ca=1, cb=0, **kw):
    return lax.dot_general(
        a, b, (((ca,), (cb,)), ((), ())), preferred_element_type=F32, **kw
    )


def kernel(
    n, dpn, chunk,
    seg, lat, rates, wqkv, wout, cot,
    out, grad,
    xbuf, wbuf, obuf, cotv, ldr, cumr, cumb, kv, intra, states, gains, mine, totals,
    sbuf, tbuf, attn, gsend, grecv, gdp, gdr,
    loc, xs, xr, xfs, xfr, ws, wr, wfs, wfr, lds, ldrs, ss, sr, ts, tr, ats, atr,
    gs, gr, ds_, dr,
):
    z = lax.axis_index("seq")
    h = lax.axis_index("head")
    d = lax.axis_index("dp")
    g = lax.axis_index("groups")
    rows, width = xbuf.shape[1], xbuf.shape[2]
    strip = lat.shape[1]
    half = xbuf.shape[3]
    tokens = rows * width
    heads = half // 128
    per_row = width // chunk
    chunks = rows * per_row
    shard = wout.shape[0]
    piece = shard // 4
    scale = 128 ** (-0.5)
    quarter = (d % 2) * 2 + g
    pair = d + 1 - 2 * (d % 2)
    partners = ({"dp": pair}, {"groups": 1 - g}, {"dp": pair, "groups": 1 - g})

    barrier = pltpu.get_barrier_semaphore()
    count = 0
    for device in (
        [{"seq": lax.rem(z + o, n)} for o in range(1, n)]
        + [{"head": 1 - h}, {"groups": 1 - g}, {"dp": pair, "groups": 1 - g}]
        + [{"dp": lax.rem(d + o, dpn)} for o in range(1, dpn)]
    ):
        pl.semaphore_signal(
            barrier, inc=1, device_id=device, device_id_type=pl.DeviceIdType.MESH
        )
        count += 1
    pl.semaphore_wait(barrier, count)

    def to(o):
        return lax.rem(z + o, n)

    def frm(o):
        return lax.rem(z + n - o, n)

    def mult(v, m):
        return pl.multiple_of(v, m)

    def xslot(src):
        return xbuf.at[h, :, pl.ds(mult(src * strip, strip), strip), :]

    def xslot_other(src):
        return xbuf.at[1 - h, :, pl.ds(mult(src * strip, strip), strip), :]

    def lat_block(dst):
        return lat.at[pl.ds(dst * rows, rows)]

    sent = []
    for o in range(1, n):
        c = remote(rates.at[to(o)], ldr.at[z], lds.at[o - 1], ldrs.at[o - 1], {"seq": to(o)})
        c.start()
        sent.append(c)
    local = [
        pltpu.make_async_copy(rates.at[z], ldr.at[z], loc.at[0]),
        pltpu.make_async_copy(lat_block(z), xslot(z), loc.at[1]),
        pltpu.make_async_copy(wqkv, wbuf.at[:, pl.ds(mult(z * shard, shard), shard), :], loc.at[2]),
        pltpu.make_async_copy(wout, obuf.at[pl.ds(mult(z * shard, shard), shard), :], loc.at[3]),
        pltpu.make_async_copy(cot, cotv, loc.at[4]),
    ]
    for o in range(1, n):
        c = remote(lat_block(to(o)), xslot(z), xs.at[o - 1], xr.at[o - 1], {"seq": to(o)})
        c.start()
        sent.append(c)

    def wsrc(a, row):
        rng = pl.ds(mult(row, piece), piece)
        return (wqkv.at[pl.ds(1, 2), rng, :], wqkv.at[0, rng, :], wout.at[rng, :])[a]

    def wdst(a, row):
        rng = pl.ds(mult(row, piece), piece)
        return (wbuf.at[pl.ds(1, 2), rng, :], wbuf.at[0, rng, :], obuf.at[rng, :])[a]

    for a in range(3):
        for o in range(1, n):
            c = remote(
                wsrc(a, quarter * piece), wdst(a, z * shard + quarter * piece),
                ws.at[a, o - 1], wr.at[a, o - 1], {"seq": to(o)},
            )
            c.start()
            sent.append(c)
    own = remote(lat_block(z), xslot(z), xfs.at[0], xfr.at[0], {"head": 1 - h})
    own.start()
    sent.append(own)
    for c in local:
        c.start()

    local[0].wait()
    for o in range(1, n):
        remote(rates.at[z], ldr.at[frm(o)], lds.at[o - 1], ldrs.at[o - 1], {"seq": frm(o)}).wait_recv()
    rate = ldr[0]
    for i in range(1, n):
        rate = rate + ldr[i]
    row_i = lax.broadcasted_iota(jnp.int32, (chunk, chunk), 0)
    col_i = lax.broadcasted_iota(jnp.int32, (chunk, chunk), 1)
    upper = jnp.where(row_i <= col_i, 1.0, 0.0).astype(F32)
    lower = jnp.where(row_i >= col_i, 1.0, 0.0).astype(F32)
    for j in range(per_row):
        part = rate[:, j * chunk:(j + 1) * chunk]
        cumr[:, j * chunk:(j + 1) * chunk] = dot(part, upper, precision=lax.Precision.HIGHEST)
        cumc = dot(lower, part, 1, 1, precision=lax.Precision.HIGHEST)
        for i in range(rows * heads):
            cumb[i, j * chunk:(j + 1) * chunk, :] = jnp.broadcast_to(cumc[:, i:i + 1], (chunk, 128))

    for o in range(1, n):
        remote(lat_block(z), xslot(frm(o)), xs.at[o - 1], xr.at[o - 1], {"seq": frm(o)}).wait_recv()
        c = remote(xslot(frm(o)), xslot(frm(o)), xfs.at[o], xfr.at[o], {"head": 1 - h})
        c.start()
        sent.append(c)

    def forward(a):
        for o in range(1, n):
            slot = wdst(a, frm(o) * shard + quarter * piece)
            remote(wsrc(a, quarter * piece), slot, ws.at[a, o - 1], wr.at[a, o - 1], {"seq": frm(o)}).wait_recv()
            for p in range(3):
                c = remote(slot, slot, wfs.at[a, o - 1, p], wfr.at[a, o - 1, p], partners[p])
                c.start()
                sent.append(c)

    other_quarter = (
        (1 - d % 2) * 2 + g, (d % 2) * 2 + 1 - g, (1 - d % 2) * 2 + 1 - g
    )

    def forwarded(a):
        for o in range(1, n):
            for p in range(3):
                slot = wdst(a, frm(o) * shard + other_quarter[p] * piece)
                remote(slot, slot, wfs.at[a, o - 1, p], wfr.at[a, o - 1, p], partners[p]).wait_recv()

    forward(0)
    forward(1)
    local[1].wait()
    local[2].wait()
    for o in range(n):
        src = z if o == 0 else frm(o)
        remote(xslot_other(src), xslot_other(src), xfs.at[o], xfr.at[o], {"head": 1 - h}).wait_recv()
    forwarded(0)

    def project(c):
        def step(i, carry):
            r, j = i // per_row, i % per_row
            at = pl.ds(mult(j * chunk, chunk), chunk)
            acc = dot(xbuf[0, r, at, :], wbuf[c, :half, :]) + dot(xbuf[1, r, at, :], wbuf[c, half:, :])
            kv[c, pl.ds(mult(i * chunk, chunk), chunk), :] = acc.astype(BF)
            return carry

        lax.fori_loop(0, chunks, step, 0)

    project(1)
    project(2)

    starts = [jnp.int32(0)]
    for j in range(seg.shape[1] - 1):
        starts.append(starts[-1] + seg[0, j])

    def seg_at(position):
        total = jnp.int32(-1)
        for s in starts:
            total = total + jnp.where(s <= position, 1, 0)
        return total

    def seg_vec(position):
        total = jnp.full(position.shape, -1, jnp.int32)
        for s in starts:
            total = total + jnp.where(position >= s, 1, 0)
        return total

    first = z * tokens
    tall = lax.broadcasted_iota(jnp.int32, (chunk, 128), 0)

    def state_head(hh, carry):
        lanes = pl.ds(mult(hh * 128, 128), 128)
        state = jnp.zeros((128, 128), F32)
        gain = jnp.ones((1, 128), F32)
        for ci in range(chunks):
            r, j = ci // per_row, ci % per_row
            base = first + ci * chunk
            cum = cumb[r * heads + hh, j * chunk:(j + 1) * chunk, :]
            last = cumb[r * heads + hh, (j + 1) * chunk - 1:(j + 1) * chunk, :]
            seg_last = seg_at(base + chunk - 1)
            tail = jnp.where(seg_vec(tall + base) == seg_last, jnp.exp(last - cum), 0.0)
            toks = pl.ds(ci * chunk, chunk)
            dk = (kv[1, toks, lanes].astype(F32) * tail).astype(BF)
            fresh = dot(dk, kv[2, toks, lanes], 0, 0)
            states[hh, ci] = state
            gains[hh, ci:ci + 1, :] = gain
            through = jnp.exp(last) * jnp.where(seg_last == seg_at(base - 1), 1.0, 0.0)
            state = state * through + fresh
            gain = gain * through
        mine[pl.ds(mult(hh * 128, 128), 128), :] = state.astype(BF)
        totals[pl.ds(hh * 8, 8), :] = jnp.broadcast_to(gain, (8, 128))
        return carry

    lax.fori_loop(0, heads, state_head, 0)

    for o in range(1, n):
        @pl.when(z + o < n)
        def _():
            remote(mine, sbuf.at[o - 1], ss.at[o - 1], sr.at[o - 1], {"seq": z + o}).start()
            remote(totals, tbuf.at[o - 1], ts.at[o - 1], tr.at[o - 1], {"seq": z + o}).start()

    forward(2)
    forwarded(1)
    project(0)

    def within(idx, carry):
        hh, ci = idx // chunks, idx % chunks
        r, j = ci // per_row, ci % per_row
        lanes = pl.ds(mult(hh * 128, 128), 128)
        toks = pl.ds(mult(ci * chunk, chunk), chunk)
        at = pl.ds(mult(j * chunk, chunk), chunk)
        base = first + ci * chunk
        cum = cumb[r * heads + hh, at, :]
        column = jnp.concatenate([cum] * (chunk // 128), axis=1)
        row = cumr[pl.ds(r * heads + hh, 1), at]
        seg_row = seg_vec(base + lax.broadcasted_iota(jnp.int32, (1, chunk), 1))
        seg_col = seg_vec(base + lax.broadcasted_iota(jnp.int32, (chunk, 1), 0))
        allowed = (row_i >= col_i) & (seg_col == seg_row)
        weight = jnp.where(allowed, jnp.exp(jnp.where(allowed, column - row, 0.0)), 0.0)
        scores = dot(kv[0, toks, lanes], kv[1, toks, lanes], 1, 1)
        mixing = (scores * scale * weight).astype(BF)
        intra[toks, lanes] = dot(mixing, kv[2, toks, lanes])
        return carry

    lax.fori_loop(0, heads * chunks, within, 0)

    for o in range(1, n):
        @pl.when(z + o < n)
        def _():
            remote(mine, sbuf.at[o - 1], ss.at[o - 1], sr.at[o - 1], {"seq": z + o}).wait_send()
            remote(totals, tbuf.at[o - 1], ts.at[o - 1], tr.at[o - 1], {"seq": z + o}).wait_send()
    for hh in range(heads):
        states[hh, chunks] = jnp.zeros((128, 128), F32)
    for o in range(n - 1, 0, -1):
        @pl.when(z - o >= 0)
        def _():
            remote(mine, sbuf.at[o - 1], ss.at[o - 1], sr.at[o - 1], {"seq": z - o}).wait_recv()
            remote(totals, tbuf.at[o - 1], ts.at[o - 1], tr.at[o - 1], {"seq": z - o}).wait_recv()
            for hh in range(heads):
                states[hh, chunks] = (
                    states[hh, chunks] * tbuf[o - 1, hh * 8:hh * 8 + 1, :]
                    + sbuf[o - 1, hh * 128:(hh + 1) * 128, :].astype(F32)
                )

    def finish(hh):
        lanes = pl.ds(hh * 128, 128)

        def step(ci, carry):
            r, j = ci // per_row, ci % per_row
            toks = pl.ds(mult(ci * chunk, chunk), chunk)
            base = first + ci * chunk
            cum = cumb[r * heads + hh, pl.ds(mult(j * chunk, chunk), chunk), :]
            state = states[hh, ci] + gains[hh, pl.ds(ci, 1), :] * states[hh, chunks]
            carried = dot(kv[0, toks, lanes], state.astype(BF))
            kept = jnp.where(seg_vec(tall + base) == seg_at(base - 1), jnp.exp(cum), 0.0)
            o = intra[toks, lanes] + kept * carried * scale
            norm = lax.rsqrt(jnp.mean(o * o, axis=1, keepdims=True) + 1e-6)
            attn[h, toks, lanes] = (o * norm).astype(BF)
            return carry

        lax.fori_loop(0, chunks, step, 0)

    for hh in range(heads):
        finish(hh)
        lanes = pl.ds(hh * 128, 128)
        c = remote(attn.at[h, :, lanes], attn.at[h, :, lanes], ats.at[hh], atr.at[hh], {"head": 1 - h})
        c.start()
        sent.append(c)

    local[4].wait()
    factor = float(dpn * n * tokens) ** (-0.5)

    def grad_half(which):
        def step(i, carry):
            lanes = pl.ds(mult(i * 128, 128), 128)
            part = dot(attn[which, :, lanes], cotv[...], 0, 0) * factor
            gsend[pl.ds(mult(which * half + i * 128, 128), 128), :] = part.astype(BF)
            return carry

        lax.fori_loop(0, heads, step, 0)

    grad_half(h)
    for hh in range(heads):
        lanes = pl.ds(hh * 128, 128)
        remote(attn.at[1 - h, :, lanes], attn.at[1 - h, :, lanes], ats.at[hh], atr.at[hh], {"head": 1 - h}).wait_recv()
    grad_half(1 - h)
    for o in range(1, n):
        c = remote(
            gsend.at[pl.ds(mult(to(o) * shard, shard), shard), :], grecv.at[o - 1],
            gs.at[o - 1], gr.at[o - 1], {"seq": to(o)},
        )
        c.start()
        sent.append(c)

    local[3].wait()
    forwarded(2)

    def out_step(i, carry):
        toks = pl.ds(mult(i * chunk, chunk), chunk)
        acc = dot(attn[0, toks, :], obuf[:half, :]) + dot(attn[1, toks, :], obuf[half:, :])
        out[toks, :] = acc.astype(BF)
        return carry

    lax.fori_loop(0, chunks, out_step, 0)

    total = gsend[pl.ds(mult(z * shard, shard), shard), :].astype(F32)
    for o in range(1, n):
        remote(gsend.at[pl.ds(0, shard), :], grecv.at[o - 1], gs.at[o - 1], gr.at[o - 1], {"seq": frm(o)}).wait_recv()
        total = total + grecv[o - 1].astype(F32)
    gdp[...] = total.astype(BF)
    gdr[d] = gdp[...]
    for o in range(1, dpn):
        peer = lax.rem(d + o, dpn)
        c = remote(gdp, gdr.at[d], ds_.at[o - 1], dr.at[o - 1], {"dp": peer})
        c.start()
        sent.append(c)
    for o in range(1, dpn):
        peer = lax.rem(d + dpn - o, dpn)
        remote(gdp, gdr.at[peer], ds_.at[o - 1], dr.at[o - 1], {"dp": peer}).wait_recv()
    total = gdr[0].astype(F32)
    for i in range(1, dpn):
        total = total + gdr[i].astype(F32)
    grad[...] = total
    for c in sent:
        c.wait_send()


def local(n, dpn, latents, log_decay, seg_lengths, qkv_weight, out_weight, cotangent):
    _, all_rows, strip, half = latents.shape
    rows = all_rows // n
    width = strip * n
    tokens = rows * width
    heads = log_decay.shape[3]
    shard = out_weight.shape[0]
    chunk = min(256, width)
    chunks = tokens // chunk
    z = lax.axis_index("seq")
    rates = jnp.transpose(log_decay[0].astype(F32), (0, 2, 1)).reshape(n, rows * heads, strip)
    column = lax.broadcasted_iota(jnp.int32, (1, 1, width), 2)
    rates = jnp.where(column // strip == z, jnp.tile(rates, (1, 1, n)), 0.0)
    wqkv = jnp.transpose(qkv_weight, (1, 0, 2))
    anyspace = pl.BlockSpec(memory_space=pl.ANY)
    vmem = pl.BlockSpec(memory_space=pltpu.VMEM)
    dma = pltpu.SemaphoreType.DMA
    m = n - 1
    out, grad = pl.pallas_call(
        partial(kernel, n, dpn, chunk),
        out_shape=(
            jax.ShapeDtypeStruct((tokens, half), BF),
            jax.ShapeDtypeStruct((shard, half), F32),
        ),
        in_specs=[pl.BlockSpec(memory_space=pltpu.SMEM)] + [anyspace] * 5,
        out_specs=(vmem, vmem),
        scratch_shapes=[
            pltpu.VMEM((2, rows, width, half), BF),
            pltpu.VMEM((3, 2 * half, half), BF),
            pltpu.VMEM((2 * half, half), BF),
            pltpu.VMEM((tokens, half), BF),
            pltpu.VMEM((n, rows * heads, width), F32),
            pltpu.VMEM((rows * heads, width), F32),
            pltpu.VMEM((rows * heads, width, 128), F32),
            pltpu.VMEM((3, tokens, half), BF),
            pltpu.VMEM((tokens, half), F32),
            pltpu.VMEM((heads, chunks + 1, 128, 128), F32),
            pltpu.VMEM((heads, chunks, 128), F32),
            pltpu.VMEM((half, 128), BF),
            pltpu.VMEM((heads * 8, 128), F32),
            pltpu.VMEM((m, half, 128), BF),
            pltpu.VMEM((m, heads * 8, 128), F32),
            pltpu.VMEM((2, tokens, half), BF),
            pltpu.VMEM((2 * half, half), BF),
            pltpu.VMEM((m, shard, half), BF),
            pltpu.VMEM((shard, half), BF),
            pltpu.VMEM((dpn, shard, half), BF),
            dma((5,)),
            dma((m,)), dma((m,)), dma((n,)), dma((n,)),
            dma((3, m)), dma((3, m)), dma((3, m, 3)), dma((3, m, 3)),
            dma((m,)), dma((m,)),
            dma((m,)), dma((m,)), dma((m,)), dma((m,)),
            dma((heads,)), dma((heads,)),
            dma((m,)), dma((m,)),
            dma((dpn - 1,)), dma((dpn - 1,)),
        ],
        compiler_params=pltpu.CompilerParams(
            collective_id=0, has_side_effects=True, vmem_limit_bytes=56 * 1024 * 1024
        ),
    )(
        seg_lengths, latents[0], rates, wqkv, out_weight,
        cotangent.reshape(tokens, half),
    )
    return out.reshape(1, rows, width, half), grad


def solution(mesh):
    from jax.sharding import PartitionSpec as P

    in_specs = (
        P(("groups", "dp"), None, "seq", "head"),
        P(("groups", "dp"), None, "seq", "head"),
        P(("groups", "dp"), None),
        P("seq", None, "head"),
        P("seq", "head"),
        P(("groups", "dp"), "seq", None, "head"),
    )
    out_specs = (P(("groups", "dp"), "seq", None, "head"), P(("groups", "seq"), "head"))
    return jax.shard_map(
        partial(local, mesh.shape["seq"], mesh.shape["dp"]),
        mesh=mesh, in_specs=in_specs, out_specs=out_specs, check_vma=False,
    )
```

```python
from functools import partial

import jax
import jax.numpy as jnp
from jax import lax
from jax.experimental import pallas as pl
from jax.experimental.pallas import tpu as pltpu

BF = jnp.bfloat16
F32 = jnp.float32


def remote(src, dst, send, recv, device):
    return pltpu.make_async_remote_copy(
        src_ref=src,
        dst_ref=dst,
        send_sem=send,
        recv_sem=recv,
        device_id=device,
        device_id_type=pl.DeviceIdType.MESH,
    )


def dot(a, b, ca=1, cb=0, **kw):
    return lax.dot_general(
        a, b, (((ca,), (cb,)), ((), ())), preferred_element_type=F32, **kw
    )


def kernel(
    n, dpn, chunk,
    seg, lat, rates, wqkv, wout, cot,
    out, grad,
    xbuf, wbuf, obuf, cotv, ldr, cumr, cumb, kv, intra, states, gains, mine, totals,
    sbuf, tbuf, attn, gsend, gpair, gz, grecv, gdp, gdr, gfin,
    loc, xs, xr, xfs, xfr, ws, wr, wfs, wfr, lds, ldrs, ss, sr, ts, tr, ats, atr,
    gps, gpr, gs, gr, ds_, dr,
):
    z = lax.axis_index("seq")
    h = lax.axis_index("head")
    d = lax.axis_index("dp")
    g = lax.axis_index("groups")
    rows, width = xbuf.shape[1], xbuf.shape[2]
    strip = lat.shape[1]
    half = xbuf.shape[3]
    tokens = rows * width
    heads = half // 128
    per_row = width // chunk
    chunks = rows * per_row
    shard = wout.shape[0]
    piece = shard // 4
    scale = 128 ** (-0.5)
    quarter = (d % 2) * 2 + g
    pair = d + 1 - 2 * (d % 2)
    partners = ({"dp": pair}, {"groups": 1 - g})

    barrier = pltpu.get_barrier_semaphore()
    count = 0
    for device in (
        [{"seq": lax.rem(z + o, n)} for o in range(1, n)]
        + [{"head": 1 - h}, {"groups": 1 - g}, {"dp": pair}]
        + [{"dp": lax.rem(d + 2 * o, dpn)} for o in range(1, dpn // 2)]
    ):
        pl.semaphore_signal(
            barrier, inc=1, device_id=device, device_id_type=pl.DeviceIdType.MESH
        )
        count += 1
    pl.semaphore_wait(barrier, count)

    def to(o):
        return lax.rem(z + o, n)

    def frm(o):
        return lax.rem(z + n - o, n)

    def mult(v, m):
        return pl.multiple_of(v, m)

    def xslot(src):
        return xbuf.at[h, :, pl.ds(mult(src * strip, strip), strip), :]

    def xslot_other(src):
        return xbuf.at[1 - h, :, pl.ds(mult(src * strip, strip), strip), :]

    def lat_block(dst):
        return lat.at[pl.ds(dst * rows, rows)]

    sent, guarded = [], []
    for o in range(1, n):
        c = remote(rates.at[to(o)], ldr.at[z], lds.at[o - 1], ldrs.at[o - 1], {"seq": to(o)})
        c.start()
        sent.append(c)
    local = [
        pltpu.make_async_copy(rates.at[z], ldr.at[z], loc.at[0]),
        pltpu.make_async_copy(lat_block(z), xslot(z), loc.at[1]),
        pltpu.make_async_copy(wqkv, wbuf.at[:, pl.ds(mult(z * shard, shard), shard), :], loc.at[2]),
        pltpu.make_async_copy(wout, obuf.at[pl.ds(mult(z * shard, shard), shard), :], loc.at[3]),
        pltpu.make_async_copy(cot, cotv, loc.at[4]),
    ]
    def send_latents():
        for o in range(1, n):
            c = remote(lat_block(to(o)), xslot(z), xs.at[o - 1], xr.at[o - 1], {"seq": to(o)})
            c.start()
            sent.append(c)

    def wsrc(a, row):
        rng = pl.ds(mult(row, piece), piece)
        return (wqkv.at[pl.ds(1, 2), rng, :], wqkv.at[0, rng, :], wout.at[rng, :])[a]

    def wdst(a, row):
        rng = pl.ds(mult(row, piece), piece)
        return (wbuf.at[pl.ds(1, 2), rng, :], wbuf.at[0, rng, :], obuf.at[rng, :])[a]

    own_part = quarter * piece

    def wslot(a, src, q):
        return wdst(a, src * shard + q * piece)

    def when(cond, make):
        @pl.when(cond)
        def _():
            make().start()

        guarded.append((cond, make))

    def launch(a):
        for way, cond, dev in ((0, z + 1 < n, z + 1), (1, z > 0, z - 1)):
            when(cond, partial(
                lambda way, dev: remote(
                    wsrc(a, own_part), wslot(a, z, quarter), ws.at[a, way, 0], wr.at[a, way, 0], {"seq": dev}
                ), way, dev))

    def each(fn):
        for s in range(1, n):
            for way in range(2):
                src = z - s if way == 0 else z + s
                has = src >= 0 if way == 0 else src < n
                fn(s, way, src, has)

    def chain(a):
        def visit(s, way, src, has):
            onward = z + 1 if way == 0 else z - 1
            more = has & (onward < n if way == 0 else onward >= 0)

            @pl.when(has)
            def _():
                slot = wslot(a, src, quarter)
                remote(slot, slot, ws.at[a, way, s - 1], wr.at[a, way, s - 1], {"seq": z}).wait_recv()

            if s < n - 1:
                when(more, lambda: remote(
                    wslot(a, src, quarter), wslot(a, src, quarter),
                    ws.at[a, way, s], wr.at[a, way, s], {"seq": onward}))
            for p in range(2):
                when(has, partial(lambda p: remote(
                    wslot(a, src, quarter), wslot(a, src, quarter),
                    wfs.at[a, way, s - 1, p], wfr.at[a, way, s - 1, p], partners[p]), p))

        each(visit)

    def cut(ref, p):
        lanes = pl.ds(p * (half // 2), half // 2)
        return ref.at[:, :, lanes] if len(ref.shape) == 3 else ref.at[:, lanes]

    def diagonal(a):
        def visit(s, way, src, has):
            for p in range(2):
                @pl.when(has)
                def _():
                    slot = wslot(a, src, other_quarter[p])
                    remote(slot, slot, wfs.at[a, way, s - 1, p], wfr.at[a, way, s - 1, p], partners[p]).wait_recv()

                when(has, partial(lambda p: remote(
                    cut(wslot(a, src, other_quarter[p]), p), cut(wslot(a, src, other_quarter[p]), p),
                    wfs.at[a, way, s - 1, 2 + p], wfr.at[a, way, s - 1, 2 + p], partners[1 - p]), p))

        each(visit)

    def settle(a):
        def visit(s, way, src, has):
            @pl.when(has)
            def _():
                for p in range(2):
                    slot = cut(wslot(a, src, other_quarter[2]), p)
                    remote(slot, slot, wfs.at[a, way, s - 1, 2 + p], wfr.at[a, way, s - 1, 2 + p], partners[1 - p]).wait_recv()

        each(visit)

    other_quarter = (
        (1 - d % 2) * 2 + g, (d % 2) * 2 + 1 - g, (1 - d % 2) * 2 + 1 - g
    )
    launch(0)
    send_latents()
    launch(1)
    launch(2)
    own = remote(lat_block(z), xslot(z), xfs.at[0], xfr.at[0], {"head": 1 - h})
    own.start()
    sent.append(own)
    for c in local:
        c.start()

    local[0].wait()
    for o in range(1, n):
        remote(rates.at[z], ldr.at[frm(o)], lds.at[o - 1], ldrs.at[o - 1], {"seq": frm(o)}).wait_recv()
    rate = ldr[0]
    for i in range(1, n):
        rate = rate + ldr[i]
    row_i = lax.broadcasted_iota(jnp.int32, (chunk, chunk), 0)
    col_i = lax.broadcasted_iota(jnp.int32, (chunk, chunk), 1)
    upper = jnp.where(row_i <= col_i, 1.0, 0.0).astype(F32)
    lower = jnp.where(row_i >= col_i, 1.0, 0.0).astype(F32)
    for j in range(per_row):
        part = rate[:, j * chunk:(j + 1) * chunk]
        cumr[:, j * chunk:(j + 1) * chunk] = dot(part, upper, precision=lax.Precision.HIGHEST)
        cumc = dot(lower, part, 1, 1, precision=lax.Precision.HIGHEST)
        for i in range(rows * heads):
            cumb[i, j * chunk:(j + 1) * chunk, :] = jnp.broadcast_to(cumc[:, i:i + 1], (chunk, 128))

    def forward_latents():
        for o in range(1, n):
            remote(lat_block(z), xslot(frm(o)), xs.at[o - 1], xr.at[o - 1], {"seq": frm(o)}).wait_recv()
            c = remote(xslot(frm(o)), xslot(frm(o)), xfs.at[o], xfr.at[o], {"head": 1 - h})
            c.start()
            sent.append(c)

    chain(0)
    chain(1)
    diagonal(0)
    forward_latents()
    diagonal(1)
    chain(2)
    settle(0)
    local[1].wait()
    local[2].wait()
    for o in range(n):
        src = z if o == 0 else frm(o)
        remote(xslot_other(src), xslot_other(src), xfs.at[o], xfr.at[o], {"head": 1 - h}).wait_recv()

    def project(c):
        def step(i, carry):
            r, j = i // per_row, i % per_row
            at = pl.ds(mult(j * chunk, chunk), chunk)
            acc = dot(xbuf[0, r, at, :], wbuf[c, :half, :]) + dot(xbuf[1, r, at, :], wbuf[c, half:, :])
            kv[c, pl.ds(mult(i * chunk, chunk), chunk), :] = acc.astype(BF)
            return carry

        lax.fori_loop(0, chunks, step, 0)

    project(1)
    project(2)

    starts = [jnp.int32(0)]
    for j in range(seg.shape[1] - 1):
        starts.append(starts[-1] + seg[0, j])

    def seg_at(position):
        total = jnp.int32(-1)
        for s in starts:
            total = total + jnp.where(s <= position, 1, 0)
        return total

    def seg_vec(position):
        total = jnp.full(position.shape, -1, jnp.int32)
        for s in starts:
            total = total + jnp.where(position >= s, 1, 0)
        return total

    first = z * tokens
    tall = lax.broadcasted_iota(jnp.int32, (chunk, 128), 0)

    def state_head(hh, carry):
        lanes = pl.ds(mult(hh * 128, 128), 128)
        state = jnp.zeros((128, 128), F32)
        gain = jnp.ones((1, 128), F32)
        for ci in range(chunks):
            r, j = ci // per_row, ci % per_row
            base = first + ci * chunk
            cum = cumb[r * heads + hh, j * chunk:(j + 1) * chunk, :]
            last = cumb[r * heads + hh, (j + 1) * chunk - 1:(j + 1) * chunk, :]
            seg_last = seg_at(base + chunk - 1)
            tail = jnp.where(seg_vec(tall + base) == seg_last, jnp.exp(last - cum), 0.0)
            toks = pl.ds(ci * chunk, chunk)
            dk = (kv[1, toks, lanes].astype(F32) * tail).astype(BF)
            fresh = dot(dk, kv[2, toks, lanes], 0, 0)
            states[hh, ci] = state
            gains[hh, ci:ci + 1, :] = gain
            through = jnp.exp(last) * jnp.where(seg_last == seg_at(base - 1), 1.0, 0.0)
            state = state * through + fresh
            gain = gain * through
        mine[pl.ds(mult(hh * 128, 128), 128), :] = state.astype(BF)
        totals[pl.ds(hh * 8, 8), :] = jnp.broadcast_to(gain, (8, 128))
        return carry

    lax.fori_loop(0, heads, state_head, 0)

    for o in range(1, n):
        @pl.when(z + o < n)
        def _():
            remote(mine, sbuf.at[o - 1], ss.at[o - 1], sr.at[o - 1], {"seq": z + o}).start()
            remote(totals, tbuf.at[o - 1], ts.at[o - 1], tr.at[o - 1], {"seq": z + o}).start()

    settle(1)
    diagonal(2)
    project(0)

    def within(idx, carry):
        hh, ci = idx // chunks, idx % chunks
        r, j = ci // per_row, ci % per_row
        lanes = pl.ds(mult(hh * 128, 128), 128)
        toks = pl.ds(mult(ci * chunk, chunk), chunk)
        at = pl.ds(mult(j * chunk, chunk), chunk)
        base = first + ci * chunk
        cum = cumb[r * heads + hh, at, :]
        column = jnp.concatenate([cum] * (chunk // 128), axis=1)
        row = cumr[pl.ds(r * heads + hh, 1), at]
        seg_row = seg_vec(base + lax.broadcasted_iota(jnp.int32, (1, chunk), 1))
        seg_col = seg_vec(base + lax.broadcasted_iota(jnp.int32, (chunk, 1), 0))
        allowed = (row_i >= col_i) & (seg_col == seg_row)
        weight = jnp.where(allowed, jnp.exp(jnp.where(allowed, column - row, 0.0)), 0.0)
        scores = dot(kv[0, toks, lanes], kv[1, toks, lanes], 1, 1)
        mixing = (scores * scale * weight).astype(BF)
        intra[toks, lanes] = dot(mixing, kv[2, toks, lanes])
        return carry

    lax.fori_loop(0, heads * chunks, within, 0)

    for o in range(1, n):
        @pl.when(z + o < n)
        def _():
            remote(mine, sbuf.at[o - 1], ss.at[o - 1], sr.at[o - 1], {"seq": z + o}).wait_send()
            remote(totals, tbuf.at[o - 1], ts.at[o - 1], tr.at[o - 1], {"seq": z + o}).wait_send()
    for hh in range(heads):
        states[hh, chunks] = jnp.zeros((128, 128), F32)
    for o in range(n - 1, 0, -1):
        @pl.when(z - o >= 0)
        def _():
            remote(mine, sbuf.at[o - 1], ss.at[o - 1], sr.at[o - 1], {"seq": z - o}).wait_recv()
            remote(totals, tbuf.at[o - 1], ts.at[o - 1], tr.at[o - 1], {"seq": z - o}).wait_recv()
            for hh in range(heads):
                states[hh, chunks] = (
                    states[hh, chunks] * tbuf[o - 1, hh * 8:hh * 8 + 1, :]
                    + sbuf[o - 1, hh * 128:(hh + 1) * 128, :].astype(F32)
                )

    def finish(hh):
        lanes = pl.ds(hh * 128, 128)

        def step(ci, carry):
            r, j = ci // per_row, ci % per_row
            toks = pl.ds(mult(ci * chunk, chunk), chunk)
            base = first + ci * chunk
            cum = cumb[r * heads + hh, pl.ds(mult(j * chunk, chunk), chunk), :]
            state = states[hh, ci] + gains[hh, pl.ds(ci, 1), :] * states[hh, chunks]
            carried = dot(kv[0, toks, lanes], state.astype(BF))
            kept = jnp.where(seg_vec(tall + base) == seg_at(base - 1), jnp.exp(cum), 0.0)
            o = intra[toks, lanes] + kept * carried * scale
            norm = lax.rsqrt(jnp.mean(o * o, axis=1, keepdims=True) + 1e-6)
            attn[h, toks, lanes] = (o * norm).astype(BF)
            return carry

        lax.fori_loop(0, chunks, step, 0)

    for hh in range(heads):
        finish(hh)
        lanes = pl.ds(hh * 128, 128)
        c = remote(attn.at[h, :, lanes], attn.at[h, :, lanes], ats.at[hh], atr.at[hh], {"head": 1 - h})
        c.start()
        sent.append(c)

    local[4].wait()
    factor = float(dpn * n * tokens) ** (-0.5)

    def grad_half(which):
        def step(i, carry):
            lanes = pl.ds(mult(i * 128, 128), 128)
            part = dot(attn[which, :, lanes], cotv[...], 0, 0) * factor
            rows_of = min(128, part_rows)
            per = shard // rows_of
            for k in range(128 // rows_of):
                at = (which * half + i * 128) // rows_of + k
                gsend[at // per, at % per, :, :] = part[k * rows_of:(k + 1) * rows_of].astype(BF)
            return carry

        lax.fori_loop(0, heads, step, 0)

    part_rows = shard // 2
    parity = d % 2
    group = n // 2

    def give(which):
        at = pl.ds(mult(which * group, group), group)
        return remote(
            gsend.at[at, 1 - parity], gpair.at[at], gps.at[which], gpr.at[which], {"dp": pair}
        )

    grad_half(h)
    give(h).start()
    for hh in range(heads):
        lanes = pl.ds(hh * 128, 128)
        remote(attn.at[1 - h, :, lanes], attn.at[1 - h, :, lanes], ats.at[hh], atr.at[hh], {"head": 1 - h}).wait_recv()
    grad_half(1 - h)
    give(1 - h).start()

    local[3].wait()
    settle(2)

    def out_step(i, carry):
        toks = pl.ds(mult(i * chunk, chunk), chunk)
        acc = dot(attn[0, toks, :], obuf[:half, :]) + dot(attn[1, toks, :], obuf[half:, :])
        out[toks, :] = acc.astype(BF)
        return carry

    lax.fori_loop(0, chunks, out_step, 0)

    give(h).wait_recv()
    give(1 - h).wait_recv()
    gz[...] = (gsend[:, parity].astype(F32) + gpair[...].astype(F32)).astype(BF)
    for o in range(1, n):
        c = remote(gz.at[to(o)], grecv.at[o - 1], gs.at[o - 1], gr.at[o - 1], {"seq": to(o)})
        c.start()
        sent.append(c)
    total = gz[z].astype(F32)
    for o in range(1, n):
        remote(gz.at[z], grecv.at[o - 1], gs.at[o - 1], gr.at[o - 1], {"seq": frm(o)}).wait_recv()
        total = total + grecv[o - 1].astype(F32)
    if dpn > 2:
        gdp[...] = total.astype(BF)
        gdr[d // 2] = gdp[...]
        for o in range(1, dpn // 2):
            c = remote(gdp, gdr.at[d // 2], ds_.at[o], dr.at[o], {"dp": lax.rem(d + 2 * o, dpn)})
            c.start()
            sent.append(c)
        for o in range(1, dpn // 2):
            peer = lax.rem(d + dpn - 2 * o, dpn)
            remote(gdp, gdr.at[peer // 2], ds_.at[o], dr.at[o], {"dp": peer}).wait_recv()
        total = gdr[0].astype(F32)
        for i in range(1, dpn // 2):
            total = total + gdr[i].astype(F32)
    gfin[parity] = total.astype(BF)
    c = remote(gfin.at[parity], gfin.at[parity], ds_.at[0], dr.at[0], {"dp": pair})
    c.start()
    remote(gfin.at[1 - parity], gfin.at[1 - parity], ds_.at[0], dr.at[0], {"dp": pair}).wait_recv()
    for i in range(2):
        grad[pl.ds(i * part_rows, part_rows), :] = gfin[i].astype(F32)
    c.wait_send()
    give(h).wait_send()
    give(1 - h).wait_send()
    for cond, make in guarded:
        @pl.when(cond)
        def _():
            make().wait_send()

    for c in sent:
        c.wait_send()


def local(n, dpn, latents, log_decay, seg_lengths, qkv_weight, out_weight, cotangent):
    _, all_rows, strip, half = latents.shape
    rows = all_rows // n
    width = strip * n
    tokens = rows * width
    heads = log_decay.shape[3]
    shard = out_weight.shape[0]
    chunk = min(256, width)
    chunks = tokens // chunk
    z = lax.axis_index("seq")
    rates = jnp.transpose(log_decay[0].astype(F32), (0, 2, 1)).reshape(n, rows * heads, strip)
    column = lax.broadcasted_iota(jnp.int32, (1, 1, width), 2)
    rates = jnp.where(column // strip == z, jnp.tile(rates, (1, 1, n)), 0.0)
    wqkv = jnp.transpose(qkv_weight, (1, 0, 2))
    anyspace = pl.BlockSpec(memory_space=pl.ANY)
    vmem = pl.BlockSpec(memory_space=pltpu.VMEM)
    dma = pltpu.SemaphoreType.DMA
    m = n - 1
    out, grad = pl.pallas_call(
        partial(kernel, n, dpn, chunk),
        out_shape=(
            jax.ShapeDtypeStruct((tokens, half), BF),
            jax.ShapeDtypeStruct((shard, half), F32),
        ),
        in_specs=[pl.BlockSpec(memory_space=pltpu.SMEM)] + [anyspace] * 5,
        out_specs=(vmem, vmem),
        scratch_shapes=[
            pltpu.VMEM((2, rows, width, half), BF),
            pltpu.VMEM((3, 2 * half, half), BF),
            pltpu.VMEM((2 * half, half), BF),
            pltpu.VMEM((tokens, half), BF),
            pltpu.VMEM((n, rows * heads, width), F32),
            pltpu.VMEM((rows * heads, width), F32),
            pltpu.VMEM((rows * heads, width, 128), F32),
            pltpu.VMEM((3, tokens, half), BF),
            pltpu.VMEM((tokens, half), F32),
            pltpu.VMEM((heads, chunks + 1, 128, 128), F32),
            pltpu.VMEM((heads, chunks, 128), F32),
            pltpu.VMEM((half, 128), BF),
            pltpu.VMEM((heads * 8, 128), F32),
            pltpu.VMEM((m, half, 128), BF),
            pltpu.VMEM((m, heads * 8, 128), F32),
            pltpu.VMEM((2, tokens, half), BF),
            pltpu.VMEM((n, 2, shard // 2, half), BF),
            pltpu.VMEM((n, shard // 2, half), BF),
            pltpu.VMEM((n, shard // 2, half), BF),
            pltpu.VMEM((m, shard // 2, half), BF),
            pltpu.VMEM((shard // 2, half), BF),
            pltpu.VMEM((dpn // 2, shard // 2, half), BF),
            pltpu.VMEM((2, shard // 2, half), BF),
            dma((5,)),
            dma((m,)), dma((m,)), dma((n,)), dma((n,)),
            dma((3, 2, m)), dma((3, 2, m)), dma((3, 2, m, 4)), dma((3, 2, m, 4)),
            dma((m,)), dma((m,)),
            dma((m,)), dma((m,)), dma((m,)), dma((m,)),
            dma((heads,)), dma((heads,)),
            dma((2,)), dma((2,)), dma((m,)), dma((m,)),
            dma((dpn // 2,)), dma((dpn // 2,)),
        ],
        compiler_params=pltpu.CompilerParams(
            collective_id=0, has_side_effects=True, vmem_limit_bytes=56 * 1024 * 1024
        ),
    )(
        seg_lengths, latents[0], rates, wqkv, out_weight,
        cotangent.reshape(tokens, half),
    )
    return out.reshape(1, rows, width, half), grad


def solution(mesh):
    from jax.sharding import PartitionSpec as P

    in_specs = (
        P(("groups", "dp"), None, "seq", "head"),
        P(("groups", "dp"), None, "seq", "head"),
        P(("groups", "dp"), None),
        P("seq", None, "head"),
        P("seq", "head"),
        P(("groups", "dp"), "seq", None, "head"),
    )
    out_specs = (P(("groups", "dp"), "seq", None, "head"), P(("groups", "seq"), "head"))
    return jax.shard_map(
        partial(local, mesh.shape["seq"], mesh.shape["dp"]),
        mesh=mesh, in_specs=in_specs, out_specs=out_specs, check_vma=False,
    )
```

```python
from functools import partial

import jax
import jax.numpy as jnp
from jax import lax
from jax.experimental import pallas as pl
from jax.experimental.pallas import tpu as pltpu

BF = jnp.bfloat16
F32 = jnp.float32


def remote(src, dst, send, recv, device):
    return pltpu.make_async_remote_copy(
        src_ref=src,
        dst_ref=dst,
        send_sem=send,
        recv_sem=recv,
        device_id=device,
        device_id_type=pl.DeviceIdType.MESH,
    )


def dot(a, b, ca=1, cb=0, **kw):
    return lax.dot_general(
        a, b, (((ca,), (cb,)), ((), ())), preferred_element_type=F32, **kw
    )


def kernel(
    n, dpn, chunk,
    seg, lat, rates, wqkv, wout, cot,
    out, grad,
    xbuf, wbuf, obuf, cotv, ldr, cumr, cumb, kv, intra, states, gains, mine, totals,
    sbuf, tbuf, attn, gsend, gpair, gz, grecv, gdp, gdr, gfin,
    loc, xs, xr, xfs, xfr, ws, wr, wfs, wfr, lds, ldrs, ss, sr, ts, tr, ats, atr,
    gps, gpr, gs, gr, ds_, dr,
):
    z = lax.axis_index("seq")
    h = lax.axis_index("head")
    d = lax.axis_index("dp")
    g = lax.axis_index("groups")
    rows, width = xbuf.shape[1], xbuf.shape[2]
    strip = lat.shape[1]
    half = xbuf.shape[3]
    tokens = rows * width
    heads = half // 128
    per_row = width // chunk
    chunks = rows * per_row
    shard = wout.shape[0]
    piece = shard // 4
    scale = 128 ** (-0.5)
    quarter = (d % 2) * 2 + g
    pair = d + 1 - 2 * (d % 2)
    partners = ({"dp": pair}, {"groups": 1 - g})

    barrier = pltpu.get_barrier_semaphore()
    count = 0
    for device in (
        [{"seq": lax.rem(z + o, n)} for o in range(1, n)]
        + [{"head": 1 - h}, {"groups": 1 - g}, {"dp": pair}]
        + [{"dp": lax.rem(d + 2 * o, dpn)} for o in range(1, dpn // 2)]
    ):
        pl.semaphore_signal(
            barrier, inc=1, device_id=device, device_id_type=pl.DeviceIdType.MESH
        )
        count += 1
    pl.semaphore_wait(barrier, count)

    def to(o):
        return lax.rem(z + o, n)

    def frm(o):
        return lax.rem(z + n - o, n)

    def mult(v, m):
        return pl.multiple_of(v, m)

    def xslot(src):
        return xbuf.at[h, :, pl.ds(mult(src * strip, strip), strip), :]

    def xslot_other(src):
        return xbuf.at[1 - h, :, pl.ds(mult(src * strip, strip), strip), :]

    def lat_block(dst):
        return lat.at[pl.ds(dst * rows, rows)]

    sent, guarded = [], []
    for o in range(1, n):
        c = remote(rates.at[to(o)], ldr.at[z], lds.at[o - 1], ldrs.at[o - 1], {"seq": to(o)})
        c.start()
        sent.append(c)
    local = [
        pltpu.make_async_copy(rates.at[z], ldr.at[z], loc.at[0]),
        pltpu.make_async_copy(lat_block(z), xslot(z), loc.at[1]),
        pltpu.make_async_copy(wqkv, wbuf.at[:, pl.ds(mult(z * shard, shard), shard), :], loc.at[2]),
        pltpu.make_async_copy(wout, obuf.at[pl.ds(mult(z * shard, shard), shard), :], loc.at[3]),
        pltpu.make_async_copy(cot, cotv, loc.at[4]),
    ]
    def send_latents():
        for o in range(1, n):
            c = remote(lat_block(to(o)), xslot(z), xs.at[o - 1], xr.at[o - 1], {"seq": to(o)})
            c.start()
            sent.append(c)

    def wsrc(a, row):
        rng = pl.ds(mult(row, piece), piece)
        return (wqkv.at[pl.ds(1, 2), rng, :], wqkv.at[0, rng, :], wout.at[rng, :])[a]

    def wdst(a, row):
        rng = pl.ds(mult(row, piece), piece)
        return (wbuf.at[pl.ds(1, 2), rng, :], wbuf.at[0, rng, :], obuf.at[rng, :])[a]

    own_part = quarter * piece

    def wslot(a, src, q):
        return wdst(a, src * shard + q * piece)

    def when(cond, make):
        @pl.when(cond)
        def _():
            make().start()

        guarded.append((cond, make))

    def launch(a):
        for way, cond, dev in ((0, z + 1 < n, z + 1), (1, z > 0, z - 1)):
            when(cond, partial(
                lambda way, dev: remote(
                    wsrc(a, own_part), wslot(a, z, quarter), ws.at[a, way, 0], wr.at[a, way, 0], {"seq": dev}
                ), way, dev))

    def each(fn):
        for s in range(1, n):
            for way in range(2):
                src = z - s if way == 0 else z + s
                has = src >= 0 if way == 0 else src < n
                fn(s, way, src, has)

    def chain(a):
        def visit(s, way, src, has):
            onward = z + 1 if way == 0 else z - 1
            more = has & (onward < n if way == 0 else onward >= 0)

            @pl.when(has)
            def _():
                slot = wslot(a, src, quarter)
                remote(slot, slot, ws.at[a, way, s - 1], wr.at[a, way, s - 1], {"seq": z}).wait_recv()

            if s < n - 1:
                when(more, lambda: remote(
                    wslot(a, src, quarter), wslot(a, src, quarter),
                    ws.at[a, way, s], wr.at[a, way, s], {"seq": onward}))
            for p in range(2):
                when(has, partial(lambda p: remote(
                    wslot(a, src, quarter), wslot(a, src, quarter),
                    wfs.at[a, way, s - 1, p], wfr.at[a, way, s - 1, p], partners[p]), p))

        each(visit)

    def cut(ref, p):
        lanes = pl.ds(p * (half // 2), half // 2)
        return ref.at[:, :, lanes] if len(ref.shape) == 3 else ref.at[:, lanes]

    def diagonal(a):
        def visit(s, way, src, has):
            for p in range(2):
                @pl.when(has)
                def _():
                    slot = wslot(a, src, other_quarter[p])
                    remote(slot, slot, wfs.at[a, way, s - 1, p], wfr.at[a, way, s - 1, p], partners[p]).wait_recv()

                when(has, partial(lambda p: remote(
                    cut(wslot(a, src, other_quarter[p]), p), cut(wslot(a, src, other_quarter[p]), p),
                    wfs.at[a, way, s - 1, 2 + p], wfr.at[a, way, s - 1, 2 + p], partners[1 - p]), p))

        each(visit)

    def settle(a):
        def visit(s, way, src, has):
            @pl.when(has)
            def _():
                for p in range(2):
                    slot = cut(wslot(a, src, other_quarter[2]), p)
                    remote(slot, slot, wfs.at[a, way, s - 1, 2 + p], wfr.at[a, way, s - 1, 2 + p], partners[1 - p]).wait_recv()

        each(visit)

    other_quarter = (
        (1 - d % 2) * 2 + g, (d % 2) * 2 + 1 - g, (1 - d % 2) * 2 + 1 - g
    )
    launch(0)
    launch(1)
    own = remote(lat_block(z), xslot(z), xfs.at[0], xfr.at[0], {"head": 1 - h})
    own.start()
    sent.append(own)
    for c in local:
        c.start()

    def forward_latents():
        for o in range(1, n):
            remote(lat_block(z), xslot(frm(o)), xs.at[o - 1], xr.at[o - 1], {"seq": frm(o)}).wait_recv()
            c = remote(xslot(frm(o)), xslot(frm(o)), xfs.at[o], xfr.at[o], {"head": 1 - h})
            c.start()
            sent.append(c)

    chain(0)
    chain(1)
    send_latents()
    launch(2)
    diagonal(0)
    diagonal(1)
    forward_latents()
    chain(2)
    settle(0)
    local[0].wait()
    for o in range(1, n):
        remote(rates.at[z], ldr.at[frm(o)], lds.at[o - 1], ldrs.at[o - 1], {"seq": frm(o)}).wait_recv()
    rate = ldr[0]
    for i in range(1, n):
        rate = rate + ldr[i]
    row_i = lax.broadcasted_iota(jnp.int32, (chunk, chunk), 0)
    col_i = lax.broadcasted_iota(jnp.int32, (chunk, chunk), 1)
    upper = jnp.where(row_i <= col_i, 1.0, 0.0).astype(F32)
    lower = jnp.where(row_i >= col_i, 1.0, 0.0).astype(F32)
    for j in range(per_row):
        part = rate[:, j * chunk:(j + 1) * chunk]
        cumr[:, j * chunk:(j + 1) * chunk] = dot(part, upper, precision=lax.Precision.HIGHEST)
        cumc = dot(lower, part, 1, 1, precision=lax.Precision.HIGHEST)
        for i in range(rows * heads):
            cumb[i, j * chunk:(j + 1) * chunk, :] = jnp.broadcast_to(cumc[:, i:i + 1], (chunk, 128))

    local[1].wait()
    local[2].wait()
    for o in range(n):
        src = z if o == 0 else frm(o)
        remote(xslot_other(src), xslot_other(src), xfs.at[o], xfr.at[o], {"head": 1 - h}).wait_recv()

    def project(c):
        def step(i, carry):
            r, j = i // per_row, i % per_row
            at = pl.ds(mult(j * chunk, chunk), chunk)
            acc = dot(xbuf[0, r, at, :], wbuf[c, :half, :]) + dot(xbuf[1, r, at, :], wbuf[c, half:, :])
            kv[c, pl.ds(mult(i * chunk, chunk), chunk), :] = acc.astype(BF)
            return carry

        lax.fori_loop(0, chunks, step, 0)

    project(1)
    project(2)

    starts = [jnp.int32(0)]
    for j in range(seg.shape[1] - 1):
        starts.append(starts[-1] + seg[0, j])

    def seg_at(position):
        total = jnp.int32(-1)
        for s in starts:
            total = total + jnp.where(s <= position, 1, 0)
        return total

    def seg_vec(position):
        total = jnp.full(position.shape, -1, jnp.int32)
        for s in starts:
            total = total + jnp.where(position >= s, 1, 0)
        return total

    first = z * tokens
    tall = lax.broadcasted_iota(jnp.int32, (chunk, 128), 0)

    def state_head(hh, carry):
        lanes = pl.ds(mult(hh * 128, 128), 128)
        state = jnp.zeros((128, 128), F32)
        gain = jnp.ones((1, 128), F32)
        for ci in range(chunks):
            r, j = ci // per_row, ci % per_row
            base = first + ci * chunk
            cum = cumb[r * heads + hh, j * chunk:(j + 1) * chunk, :]
            last = cumb[r * heads + hh, (j + 1) * chunk - 1:(j + 1) * chunk, :]
            seg_last = seg_at(base + chunk - 1)
            tail = jnp.where(seg_vec(tall + base) == seg_last, jnp.exp(last - cum), 0.0)
            toks = pl.ds(ci * chunk, chunk)
            dk = (kv[1, toks, lanes].astype(F32) * tail).astype(BF)
            fresh = dot(dk, kv[2, toks, lanes], 0, 0)
            states[hh, ci] = state
            gains[hh, ci:ci + 1, :] = gain
            through = jnp.exp(last) * jnp.where(seg_last == seg_at(base - 1), 1.0, 0.0)
            state = state * through + fresh
            gain = gain * through
        mine[pl.ds(mult(hh * 128, 128), 128), :] = state.astype(BF)
        totals[pl.ds(hh * 8, 8), :] = jnp.broadcast_to(gain, (8, 128))
        return carry

    lax.fori_loop(0, heads, state_head, 0)

    for o in range(1, n):
        @pl.when(z + o < n)
        def _():
            remote(mine, sbuf.at[o - 1], ss.at[o - 1], sr.at[o - 1], {"seq": z + o}).start()
            remote(totals, tbuf.at[o - 1], ts.at[o - 1], tr.at[o - 1], {"seq": z + o}).start()

    settle(1)
    diagonal(2)
    project(0)

    def within(idx, carry):
        hh, ci = idx // chunks, idx % chunks
        r, j = ci // per_row, ci % per_row
        lanes = pl.ds(mult(hh * 128, 128), 128)
        toks = pl.ds(mult(ci * chunk, chunk), chunk)
        at = pl.ds(mult(j * chunk, chunk), chunk)
        base = first + ci * chunk
        cum = cumb[r * heads + hh, at, :]
        column = jnp.concatenate([cum] * (chunk // 128), axis=1)
        row = cumr[pl.ds(r * heads + hh, 1), at]
        seg_row = seg_vec(base + lax.broadcasted_iota(jnp.int32, (1, chunk), 1))
        seg_col = seg_vec(base + lax.broadcasted_iota(jnp.int32, (chunk, 1), 0))
        allowed = (row_i >= col_i) & (seg_col == seg_row)
        weight = jnp.where(allowed, jnp.exp(jnp.where(allowed, column - row, 0.0)), 0.0)
        scores = dot(kv[0, toks, lanes], kv[1, toks, lanes], 1, 1)
        mixing = (scores * scale * weight).astype(BF)
        intra[toks, lanes] = dot(mixing, kv[2, toks, lanes])
        return carry

    lax.fori_loop(0, heads * chunks, within, 0)

    for o in range(1, n):
        @pl.when(z + o < n)
        def _():
            remote(mine, sbuf.at[o - 1], ss.at[o - 1], sr.at[o - 1], {"seq": z + o}).wait_send()
            remote(totals, tbuf.at[o - 1], ts.at[o - 1], tr.at[o - 1], {"seq": z + o}).wait_send()
    for hh in range(heads):
        states[hh, chunks] = jnp.zeros((128, 128), F32)
    for o in range(n - 1, 0, -1):
        @pl.when(z - o >= 0)
        def _():
            remote(mine, sbuf.at[o - 1], ss.at[o - 1], sr.at[o - 1], {"seq": z - o}).wait_recv()
            remote(totals, tbuf.at[o - 1], ts.at[o - 1], tr.at[o - 1], {"seq": z - o}).wait_recv()
            for hh in range(heads):
                states[hh, chunks] = (
                    states[hh, chunks] * tbuf[o - 1, hh * 8:hh * 8 + 1, :]
                    + sbuf[o - 1, hh * 128:(hh + 1) * 128, :].astype(F32)
                )

    def finish(hh):
        lanes = pl.ds(hh * 128, 128)

        def step(ci, carry):
            r, j = ci // per_row, ci % per_row
            toks = pl.ds(mult(ci * chunk, chunk), chunk)
            base = first + ci * chunk
            cum = cumb[r * heads + hh, pl.ds(mult(j * chunk, chunk), chunk), :]
            state = states[hh, ci] + gains[hh, pl.ds(ci, 1), :] * states[hh, chunks]
            carried = dot(kv[0, toks, lanes], state.astype(BF))
            kept = jnp.where(seg_vec(tall + base) == seg_at(base - 1), jnp.exp(cum), 0.0)
            o = intra[toks, lanes] + kept * carried * scale
            norm = lax.rsqrt(jnp.mean(o * o, axis=1, keepdims=True) + 1e-6)
            attn[h, toks, lanes] = (o * norm).astype(BF)
            return carry

        lax.fori_loop(0, chunks, step, 0)

    for hh in range(heads):
        finish(hh)
        lanes = pl.ds(hh * 128, 128)
        c = remote(attn.at[h, :, lanes], attn.at[h, :, lanes], ats.at[hh], atr.at[hh], {"head": 1 - h})
        c.start()
        sent.append(c)

    local[4].wait()
    factor = float(dpn * n * tokens) ** (-0.5)

    def grad_half(which):
        def step(i, carry):
            lanes = pl.ds(mult(i * 128, 128), 128)
            part = dot(attn[which, :, lanes], cotv[...], 0, 0) * factor
            rows_of = min(128, part_rows)
            per = shard // rows_of
            for k in range(128 // rows_of):
                at = (which * half + i * 128) // rows_of + k
                gsend[at // per, at % per, :, :] = part[k * rows_of:(k + 1) * rows_of].astype(BF)
            return carry

        lax.fori_loop(0, heads, step, 0)

    part_rows = shard // 2
    parity = d % 2
    group = n // 2

    def give(which):
        at = pl.ds(mult(which * group, group), group)
        return remote(
            gsend.at[at, 1 - parity], gpair.at[at], gps.at[which], gpr.at[which], {"dp": pair}
        )

    grad_half(h)
    give(h).start()
    for hh in range(heads):
        lanes = pl.ds(hh * 128, 128)
        remote(attn.at[1 - h, :, lanes], attn.at[1 - h, :, lanes], ats.at[hh], atr.at[hh], {"head": 1 - h}).wait_recv()
    grad_half(1 - h)
    give(1 - h).start()

    def pass_on(which):
        give(which).wait_recv()
        at = pl.ds(mult(which * group, group), group)
        gz[at] = (gsend[at, parity].astype(F32) + gpair[at].astype(F32)).astype(BF)
        for k in range(group):
            block = which * group + k
            o = lax.rem(block - z + n, n)
            slot = jnp.maximum(o - 1, 0)
            when(o > 0, partial(lambda block, slot: remote(
                gz.at[block], grecv.at[slot], gs.at[slot], gr.at[slot], {"seq": block}), block, slot))

    pass_on(h)
    local[3].wait()
    settle(2)

    def out_step(i, carry):
        toks = pl.ds(mult(i * chunk, chunk), chunk)
        acc = dot(attn[0, toks, :], obuf[:half, :]) + dot(attn[1, toks, :], obuf[half:, :])
        out[toks, :] = acc.astype(BF)
        return carry

    lax.fori_loop(0, chunks, out_step, 0)

    pass_on(1 - h)
    total = gz[z].astype(F32)
    for o in range(1, n):
        remote(gz.at[z], grecv.at[o - 1], gs.at[o - 1], gr.at[o - 1], {"seq": frm(o)}).wait_recv()
        total = total + grecv[o - 1].astype(F32)
    if dpn > 2:
        gdp[...] = total.astype(BF)
        gdr[d // 2] = gdp[...]
        for o in range(1, dpn // 2):
            c = remote(gdp, gdr.at[d // 2], ds_.at[o], dr.at[o], {"dp": lax.rem(d + 2 * o, dpn)})
            c.start()
            sent.append(c)
        for o in range(1, dpn // 2):
            peer = lax.rem(d + dpn - 2 * o, dpn)
            remote(gdp, gdr.at[peer // 2], ds_.at[o], dr.at[o], {"dp": peer}).wait_recv()
        total = gdr[0].astype(F32)
        for i in range(1, dpn // 2):
            total = total + gdr[i].astype(F32)
    gfin[parity] = total.astype(BF)
    c = remote(gfin.at[parity], gfin.at[parity], ds_.at[0], dr.at[0], {"dp": pair})
    c.start()
    remote(gfin.at[1 - parity], gfin.at[1 - parity], ds_.at[0], dr.at[0], {"dp": pair}).wait_recv()
    for i in range(2):
        grad[pl.ds(i * part_rows, part_rows), :] = gfin[i].astype(F32)
    c.wait_send()
    give(h).wait_send()
    give(1 - h).wait_send()
    for cond, make in guarded:
        @pl.when(cond)
        def _():
            make().wait_send()

    for c in sent:
        c.wait_send()


def local(n, dpn, latents, log_decay, seg_lengths, qkv_weight, out_weight, cotangent):
    _, all_rows, strip, half = latents.shape
    rows = all_rows // n
    width = strip * n
    tokens = rows * width
    heads = log_decay.shape[3]
    shard = out_weight.shape[0]
    chunk = min(256, width)
    chunks = tokens // chunk
    z = lax.axis_index("seq")
    rates = jnp.transpose(log_decay[0].astype(F32), (0, 2, 1)).reshape(n, rows * heads, strip)
    column = lax.broadcasted_iota(jnp.int32, (1, 1, width), 2)
    rates = jnp.where(column // strip == z, jnp.tile(rates, (1, 1, n)), 0.0)
    wqkv = jnp.transpose(qkv_weight, (1, 0, 2))
    anyspace = pl.BlockSpec(memory_space=pl.ANY)
    vmem = pl.BlockSpec(memory_space=pltpu.VMEM)
    dma = pltpu.SemaphoreType.DMA
    m = n - 1
    out, grad = pl.pallas_call(
        partial(kernel, n, dpn, chunk),
        out_shape=(
            jax.ShapeDtypeStruct((tokens, half), BF),
            jax.ShapeDtypeStruct((shard, half), F32),
        ),
        in_specs=[pl.BlockSpec(memory_space=pltpu.SMEM)] + [anyspace] * 5,
        out_specs=(vmem, vmem),
        scratch_shapes=[
            pltpu.VMEM((2, rows, width, half), BF),
            pltpu.VMEM((3, 2 * half, half), BF),
            pltpu.VMEM((2 * half, half), BF),
            pltpu.VMEM((tokens, half), BF),
            pltpu.VMEM((n, rows * heads, width), F32),
            pltpu.VMEM((rows * heads, width), F32),
            pltpu.VMEM((rows * heads, width, 128), F32),
            pltpu.VMEM((3, tokens, half), BF),
            pltpu.VMEM((tokens, half), F32),
            pltpu.VMEM((heads, chunks + 1, 128, 128), F32),
            pltpu.VMEM((heads, chunks, 128), F32),
            pltpu.VMEM((half, 128), BF),
            pltpu.VMEM((heads * 8, 128), F32),
            pltpu.VMEM((m, half, 128), BF),
            pltpu.VMEM((m, heads * 8, 128), F32),
            pltpu.VMEM((2, tokens, half), BF),
            pltpu.VMEM((n, 2, shard // 2, half), BF),
            pltpu.VMEM((n, shard // 2, half), BF),
            pltpu.VMEM((n, shard // 2, half), BF),
            pltpu.VMEM((m, shard // 2, half), BF),
            pltpu.VMEM((shard // 2, half), BF),
            pltpu.VMEM((dpn // 2, shard // 2, half), BF),
            pltpu.VMEM((2, shard // 2, half), BF),
            dma((5,)),
            dma((m,)), dma((m,)), dma((n,)), dma((n,)),
            dma((3, 2, m)), dma((3, 2, m)), dma((3, 2, m, 4)), dma((3, 2, m, 4)),
            dma((m,)), dma((m,)),
            dma((m,)), dma((m,)), dma((m,)), dma((m,)),
            dma((heads,)), dma((heads,)),
            dma((2,)), dma((2,)), dma((m,)), dma((m,)),
            dma((dpn // 2,)), dma((dpn // 2,)),
        ],
        compiler_params=pltpu.CompilerParams(
            collective_id=0, has_side_effects=True, vmem_limit_bytes=56 * 1024 * 1024
        ),
    )(
        seg_lengths, latents[0], rates, wqkv, out_weight,
        cotangent.reshape(tokens, half),
    )
    return out.reshape(1, rows, width, half), grad


def solution(mesh):
    from jax.sharding import PartitionSpec as P

    in_specs = (
        P(("groups", "dp"), None, "seq", "head"),
        P(("groups", "dp"), None, "seq", "head"),
        P(("groups", "dp"), None),
        P("seq", None, "head"),
        P("seq", "head"),
        P(("groups", "dp"), "seq", None, "head"),
    )
    out_specs = (P(("groups", "dp"), "seq", None, "head"), P(("groups", "seq"), "head"))
    return jax.shard_map(
        partial(local, mesh.shape["seq"], mesh.shape["dp"]),
        mesh=mesh, in_specs=in_specs, out_specs=out_specs, check_vma=False,
    )
```
